32 devices in a mesh: runs: 2 (over y), slab: 4 (over z), beads: 2 (over x), sub: 2 (over core).
Axes of the slice: x: 2, y: 2, z: 4, core: 2. Of those that a mesh axis runs over, the one named last changes fastest.
Arguments:
- dest_slab: int32 [131072, 1], P(('runs', 'slab', 'beads', 'sub')), parts along dimension 0, may hold values from 0 to 3; in each aligned block of 4096 rows (0 to 4095, 4096 to 8191, ...) at most 2048 rows name the same one
- local_cell: int32 [131072], P(('runs', 'slab', 'beads', 'sub')), parts along dimension 0, may hold values from 0 to 65535
- species: int32 [131072], P(('runs', 'slab', 'beads', 'sub')), parts along dimension 0, may hold values from 0 to 3
- bead_mass: float32 [131072], P(('runs', 'slab', 'beads', 'sub')), parts along dimension 0, may hold values from 0.5 to 1.5
- rise_fraction: float32 [131072], P(('runs', 'slab', 'beads', 'sub')), parts along dimension 0, may hold values from 0 to 1
- chi_matrix: float32 [4, 4], replicated, may hold values from 0 to 3
Outputs:
- potential: float32 [8, 8, 256, 128], P('runs', 'slab', ('beads', 'sub')), parts along dimension 0
- force: float32 [3, 8, 8, 256, 128], P(None, 'runs', 'slab', ('beads', 'sub')), parts along dimension 1
The draws below stay inside these ranges and needn't reach their ends.
There are 2 independent parts, one for each index of `runs`. The reference program is written for one: setup_inputs(seed, part) draws one part's arguments, and reference() takes and returns one part's arrays. A program takes and returns all parts, laid end to end along the dimension named above; an argument that names none is the same for every part. Nothing has to cross between parts.
Inputs may be any that keep to these rules, and one draw needn't show every extreme that they name: `dest_slab`: among the 4096 beads of one device, no slab is named more than 2048 times, a bound that some block reaches.
All inputs are finite; a program needn't handle non-finite values.
Results may differ from the reference program's by a relative error of at most 0.0003.
Values sent between devices are 32-bit elements; how exact they have to be, the bound alone decides.
No kernel may reach another device: no remote copies, remote signals or barrier semaphores. Data moves between devices by JAX's collectives and lax.ppermute only.
A program may use at most 64 MiB of HBM per device.

```python
import math
import jax
import jax.numpy as jnp
import numpy as np
from jax import lax

S = 4
X = 256
Y = 128
CZ = 2
NB_DEV = 4096
SLABS = 4
CAP = 2048
NZ = 8
BEADS = 65536


def with_ends(result, stream_key, least, top_value):
    longest = result.shape.index(max(result.shape))
    spots = []
    for shift in (0, 1):
        where = [jax.random.randint(jax.random.fold_in(stream_key, axis), (), 0, length) for axis, length in enumerate(result.shape)]
        where[longest] = (where[longest] + shift) % result.shape[longest]
        spots.append(tuple(where))
    return result.at[spots[0]].set(least).at[spots[1]].set(top_value)


def levels(stream_key, extent, split, least, top_value):
    gain = 1.0
    for position, shards_of in split:
        draws = jax.random.uniform(jax.random.fold_in(jax.random.fold_in(stream_key, 6), position), (shards_of,), jnp.float32, least / len(split), top_value / len(split))
        gain = gain * jnp.repeat(jnp.exp(draws), extent[position] // shards_of).reshape((-1,) + (1,) * (len(extent) - 1 - position))
    return gain


def routed_block(rng, own, number, rows, amount, top, most, skew):
    ranking = jax.random.permutation(rng, amount)
    crowded, usual = portions_of(amount, rows * top, most, skew, True), portions_of(amount, rows * top, most, skew, False)
    places = jnp.arange(amount)

    def named(lengths, turn):
        used = int((lengths > 0).sum())
        fixed = max(1, used // 4)
        passed = fixed + (places - fixed + turn * (used - fixed)) % max(1, amount - fixed)
        return jnp.zeros((amount,), jnp.int32).at[ranking[jnp.where(places < fixed, places, passed)]].set(jnp.asarray(lengths, jnp.int32))

    lengths = jnp.where(number % 4 == 0, named(crowded, number // 4), named(usual, number - number // 4 - 1))
    mixed = jax.random.permutation(jax.random.fold_in(own, 3), amount)
    donor, taker = mixed[0:amount // 2 * 2:2], mixed[1:amount // 2 * 2:2]
    slack = jnp.minimum(lengths[donor] - 1, most - lengths[taker]) // 2
    slack = jnp.where((donor == ranking[0]) | (taker == ranking[0]) | (lengths[taker] == 0), 0, jnp.maximum(slack, 0))
    passed = jax.random.randint(jax.random.fold_in(own, 4), (amount // 2,), 0, 1 << 20) % (slack + 1)
    lengths = lengths.at[donor].add(-passed).at[taker].add(passed)
    members = jnp.searchsorted(jnp.cumsum(lengths), jnp.arange(rows * top), side="right").astype(jnp.int32)
    table = members.reshape(top, rows).T
    table = table[jax.random.permutation(jax.random.fold_in(own, 1), rows)]
    turn = jax.random.randint(jax.random.fold_in(own, 2), (rows, 1), 0, top)
    return jnp.take_along_axis(table, (jnp.arange(top)[None, :] + turn) % top, axis=1)


def portions_of(count, total, most, skew, full):
    weights = [(1 << 20) // math.isqrt(rank ** skew) + 1 for rank in range(1, count + 1)]
    largest = most if full else min(most, max(-(-total // count), total * weights[0] // sum(weights)))
    least = 1 if total - largest >= count - 1 else 0
    given, spare = [largest] + [least] * (count - 1), total - largest - least * (count - 1)
    while spare > 0:
        free = [i for i in range(1, count) if given[i] < largest] or [i for i in range(1, count) if given[i] < most]
        mass, budget = sum([weights[i] for i in free]), spare
        for i in free:
            more = min(most - given[i], max(1, budget * weights[i] // mass), spare)
            given[i] = given[i] + more
            spare = spare - more
    return np.array(given)


def setup_inputs(seed: int = 0, part: int = 0) -> dict:
    splits = jax.random.split(jax.random.key(seed), 7)
    part_splits = jax.random.split(jax.random.fold_in(splits[6], part), 7)
    dest_slab_keys = jax.random.split(jax.random.fold_in(part_splits[0], 1), BEADS // NB_DEV)
    dest_slab_turns = jax.random.permutation(jax.random.fold_in(part_splits[0], 3), BEADS // NB_DEV)
    dest_slab = jax.vmap(lambda own, number: routed_block(jax.random.fold_in(part_splits[0], 2), own, number, NB_DEV, SLABS, 1, CAP, 2))(dest_slab_keys, dest_slab_turns).reshape((BEADS, 1))
    local_cell = with_ends(jax.random.randint(part_splits[1], (BEADS,), 0, CZ * X * Y), jax.random.fold_in(part_splits[1], 1), 0, (CZ * X * Y) - 1).astype(jnp.int32)
    species = with_ends(jax.random.randint(part_splits[2], (BEADS,), 0, S), jax.random.fold_in(part_splits[2], 1), 0, S - 1).astype(jnp.int32)
    bead_mass = jnp.clip(0.5 + 1.0 * jax.random.uniform(part_splits[3], (BEADS,), jnp.float32) ** levels(part_splits[3], (BEADS,), ((0, 16),), -0.2, 0.2), 0.5, 1.5)
    rise_fraction = jnp.clip(1.0 * jax.random.uniform(part_splits[4], (BEADS,), jnp.float32) ** levels(part_splits[4], (BEADS,), ((0, 16),), -0.2, 0.2), 0.0, 1.0)
    chi_matrix = jnp.clip(jax.random.uniform(splits[5], (S, S), jnp.float32, 0.0, 3.0), 0.0, 3.0)
    return {"dest_slab": dest_slab, "local_cell": local_cell, "species": species, "bead_mass": bead_mass, "rise_fraction": rise_fraction, "chi_matrix": chi_matrix}


compress = 0.5


def smooth_roll(values, along):
    near = jnp.roll(values, 1, along) + jnp.roll(values, -1, along)
    far = jnp.roll(values, 2, along) + jnp.roll(values, -2, along)
    return 0.375 * values + 0.25 * near + 0.0625 * far


def reference(dest_slab, local_cell, species, bead_mass, rise_fraction, chi_matrix):
    plane_cells = X * Y
    layer_index = local_cell // plane_cells
    remainder = local_cell % plane_cells
    lower_z = dest_slab[:, 0] * CZ + layer_index
    upper_z = (lower_z + 1) % NZ
    base_index = species * (NZ * plane_cells) + remainder
    lower_mass = bead_mass * (1.0 - rise_fraction)
    upper_mass = bead_mass * rise_fraction
    density = jnp.zeros((S * NZ * plane_cells,), jnp.float32)
    density = density.at[base_index + lower_z * plane_cells].add(lower_mass)
    density = density.at[base_index + upper_z * plane_cells].add(upper_mass)
    density = density.reshape(S, NZ, X, Y)
    mean_density = BEADS / (NZ * X * Y)
    smooth = density / mean_density
    smooth = smooth_roll(smooth, 1)
    smooth = smooth_roll(smooth, 2)
    smooth = smooth_roll(smooth, 3)
    coupling = 0.5 * (chi_matrix + chi_matrix.T)
    potential = jnp.einsum("ab,bzxy->azxy", coupling, smooth, precision=lax.Precision.HIGHEST)
    potential = potential + (jnp.sum(smooth, 0) - 1.0) / compress
    force = jnp.stack([-(jnp.roll(potential, -1, along) - jnp.roll(potential, 1, along)) * 0.5 for along in (1, 2, 3)])
    return potential, force
```

```python
import functools

import jax
import jax.numpy as jnp
from jax import lax
from jax.experimental import pallas as pl
from jax.experimental.pallas import tpu as pltpu
from jax.sharding import PartitionSpec as P

S = 4
X = 256
Y = 128
CZ = 2

compress = 0.5

BUCKET = 8
BUCKETS = X // BUCKET
RIM = 4
CHUNK = 256
BLOCK_LISTS = 16
TOGETHER = 4
WINDOW_BUCKETS = 3
WINDOW = WINDOW_BUCKETS * BUCKET

NT = (((1,), (1,)), ((), ()))


def pieces_of(values):
    parts = []
    for _ in range(2):
        part = values.astype(jnp.bfloat16)
        parts.append(part)
        values = values - part.astype(jnp.float32)
    parts.append(values.astype(jnp.bfloat16))
    return parts


def sort_kernel(heights, scale, dest_ref, cell_ref, species_ref, mass_ref, rise_ref, out_ref, left_ref, right_ref):
    lines = cell_ref.shape[0]
    places = lines * 128
    chunks = places // CHUNK
    cell = cell_ref[...]
    row = (cell // Y) % X
    height = dest_ref[...] * CZ + cell // (X * Y)
    key = (species_ref[...] * heights + height) * (X * Y) + cell % (X * Y)
    mass = mass_ref[...] * scale
    lower = mass * (1.0 - rise_ref[...])
    upper = mass * rise_ref[...]
    bucket = ((row + RIM) % X) // BUCKET
    member_iota = lax.broadcasted_iota(jnp.int32, (BUCKETS, 128), 0)
    members = [
        jnp.where(bucket[i : i + 1, :] == member_iota, 1.0, 0.0) for i in range(lines)
    ]
    stacked = jnp.concatenate([m.astype(jnp.bfloat16) for m in members], 0)
    source = lax.broadcasted_iota(jnp.int32, (128, 256), 0)
    target = lax.broadcasted_iota(jnp.int32, (128, 256), 1)
    before = jnp.where(source < target, 1.0, 0.0).astype(jnp.bfloat16)
    counted = jnp.dot(stacked, before, preferred_element_type=jnp.float32)
    total = jnp.zeros((BUCKETS, 128), jnp.float32)
    ranks = []
    for i in range(lines):
        ranks.append(counted[i * BUCKETS : (i + 1) * BUCKETS, :128] + total)
        total = total + counted[i * BUCKETS : (i + 1) * BUCKETS, 128:]
    start = total
    shift = 1
    while shift < BUCKETS:
        start = start + jnp.where(member_iota >= shift, pltpu.roll(start, shift, 0), 0.0)
        shift *= 2
    start = start - total
    lane = lax.broadcasted_iota(jnp.int32, (BUCKETS, 128), 1)
    starts = jnp.sum(jnp.where(member_iota == lane, start, 0.0), 0, keepdims=True)
    starts = jnp.where(lane[:1] < BUCKETS, starts, float(places))
    key_parts = [
        part.astype(jnp.float32).astype(jnp.bfloat16) for part in (key // 65536, (key // 256) % 256, key % 256)
    ]
    parts = key_parts + pieces_of(lower) + pieces_of(upper)
    parts = [part.astype(jnp.float32) for part in parts]
    chunk_iota = lax.broadcasted_iota(jnp.int32, (chunks, 128), 0)
    slot_iota = lax.broadcasted_iota(jnp.int32, (CHUNK, 128), 0)
    for i in range(lines):
        place = jnp.sum(members[i] * (ranks[i] + start), 0, keepdims=True).astype(jnp.int32)
        hit = chunk_iota == place // CHUNK
        for n, part in enumerate(parts):
            left_ref[n * chunks : (n + 1) * chunks, i * 128 : (i + 1) * 128] = jnp.where(
                hit, part[i : i + 1, :], 0.0
            ).astype(jnp.bfloat16)
        right_ref[:, i * 128 : (i + 1) * 128] = jnp.where(
            slot_iota == place % CHUNK, 1.0, 0.0
        ).astype(jnp.bfloat16)
    placed = lax.dot_general(
        left_ref[...], right_ref[...], NT, preferred_element_type=jnp.float32
    )

    def part_of(n):
        return placed[n * chunks : (n + 1) * chunks]

    out_ref[0:chunks] = part_of(0) * 65536.0 + part_of(1) * 256.0 + part_of(2)
    out_ref[chunks : 2 * chunks] = part_of(3) + part_of(4) + part_of(5)
    out_ref[2 * chunks : 3 * chunks] = part_of(6) + part_of(7) + part_of(8)
    out_ref[3 * chunks : 3 * chunks + 8] = jnp.broadcast_to(
        jnp.concatenate([starts, starts], 1), (8, CHUNK)
    )


def grid_kernel(
    heights,
    own_rows,
    chi_ref,
    place_ref,
    lists_ref,
    potential_ref,
    force_ref,
    near_ref,
    column_ref,
    amount_ref,
    starts_ref,
    starts_smem,
    grid_ref,
    sem,
):
    lists = lists_ref.shape[0]
    chunks = (lists_ref.shape[1] - 8) // 3
    places = chunks * CHUNK
    windows = -(-(own_rows // BUCKET + 1) // WINDOW_BUCKETS)
    slab = place_ref[0]
    group = place_ref[1]
    step = pl.program_id(0)

    starts_ref[...] = lists_ref[:, 3 * chunks, :128].astype(jnp.int32)
    copy = pltpu.make_async_copy(starts_ref, starts_smem, sem)
    copy.start()

    @pl.when(step == 0)
    def _():
        grid_ref[...] = jnp.zeros_like(grid_ref)

    first_row = group * own_rows - RIM

    def spread(i, carry):
        key = lists_ref[i, 0:chunks, :].astype(jnp.int32)
        lower = lists_ref[i, chunks : 2 * chunks, :]
        upper = lists_ref[i, 2 * chunks : 3 * chunks, :]
        spot = pl.ds(pl.multiple_of(i * chunks, chunks), chunks)
        species = key // (heights * X * Y)
        height = (key // (X * Y)) % heights
        row = (key // Y) % X
        near_ref[spot, :] = (row - first_row + X) % X + (species // 2) * 1024
        column_ref[spot, :] = key % Y + (species % 2) * Y
        shares = (
            0.0625 * lower,
            0.25 * lower + 0.0625 * upper,
            0.375 * lower + 0.25 * upper,
            0.25 * lower + 0.375 * upper,
            0.0625 * lower + 0.25 * upper,
            0.0625 * upper,
        )
        for n in range(CZ + 2):
            above = (slab * CZ - 1 + n + 2 + heights - height) % heights
            amount = jnp.zeros_like(lower)
            for d, share in enumerate(shares):
                amount = jnp.where(above == d, share, amount)
            high = amount.astype(jnp.bfloat16).astype(jnp.float32)
            amount_ref[2 * n, spot, :] = high
            amount_ref[2 * n + 1, spot, :] = amount - high
        return carry

    lax.fori_loop(0, lists, spread, 0)
    copy.wait()

    near_iota = lax.broadcasted_iota(jnp.int32, (2 * WINDOW, CHUNK), 0)
    near_iota = jnp.where(near_iota >= WINDOW, near_iota + (1024 - WINDOW), near_iota)
    column_iota = lax.broadcasted_iota(jnp.int32, (2 * Y, CHUNK), 0)

    def window_body(window, carry):
        def some_lists(some, carry):
            firsts, counts = [], []
            for u in range(TOGETHER):
                i = some * TOGETHER + u
                low = group * (own_rows // BUCKET) + window * WINDOW_BUCKETS
                high = low + WINDOW_BUCKETS
                wrapped = jnp.where(high > BUCKETS, BUCKETS, 0)
                begin = starts_smem[i, low]
                end = starts_smem[i, high - wrapped] + jnp.where(high > BUCKETS, places, 0)
                first = begin // CHUNK
                count = jnp.where(end > begin, (end + CHUNK - 1) // CHUNK - first, 0)
                firsts.append(first)
                counts.append(jnp.minimum(count, chunks))
            longest = functools.reduce(jnp.maximum, counts)

            def one_round(turn, carry):
                lefts, rights = [], []
                for u in range(TOGETHER):
                    line = (some * TOGETHER + u) * chunks + (firsts[u] + turn) % chunks
                    at = pl.ds(line, 1)
                    base = jnp.where(turn < counts[u], window * WINDOW, 8192)
                    hit = jnp.where(near_ref[at, :] - base == near_iota, 1.0, 0.0)
                    hit = hit.astype(jnp.bfloat16)
                    lefts.append(
                        jnp.concatenate(
                            [
                                hit * jnp.broadcast_to(amount_ref[n, at, :], hit.shape).astype(jnp.bfloat16)
                                for n in range(2 * (CZ + 2))
                            ],
                            0,
                        )
                    )
                    rights.append(
                        jnp.where(column_ref[at, :] == column_iota, 1.0, 0.0).astype(jnp.bfloat16)
                    )
                got = lax.dot_general(
                    jnp.concatenate(lefts, 1),
                    jnp.concatenate(rights, 1),
                    NT,
                    preferred_element_type=jnp.float32,
                )
                for n in range(CZ + 2):
                    for half in range(2):
                        at_high = (2 * n * 2 + half) * WINDOW
                        at_low = ((2 * n + 1) * 2 + half) * WINDOW
                        where = pl.ds(pl.multiple_of(window * WINDOW, BUCKET), WINDOW)
                        grid_ref[n, half, where, :] += (
                            got[at_high : at_high + WINDOW] + got[at_low : at_low + WINDOW]
                        )
                return carry

            return lax.fori_loop(0, longest, one_round, carry)

        return lax.fori_loop(0, lists // TOGETHER, some_lists, carry)

    lax.fori_loop(0, windows, window_body, 0)

    @pl.when(step == pl.num_programs(0) - 1)
    def _():
        rows = own_rows + 2

        def smooth_of(n, b):
            lanes = slice((b % 2) * Y, (b % 2 + 1) * Y)

            def shifted(k):
                return grid_ref[n, b // 2, RIM - 3 + k : RIM - 3 + k + rows, lanes]

            value = (
                0.375 * shifted(2) + 0.25 * (shifted(1) + shifted(3)) + 0.0625 * (shifted(0) + shifted(4))
            )
            close = pltpu.roll(value, 1, 1) + pltpu.roll(value, Y - 1, 1)
            far = pltpu.roll(value, 2, 1) + pltpu.roll(value, Y - 2, 1)
            return 0.375 * value + 0.25 * close + 0.0625 * far

        layers = []
        for n in range(CZ + 2):
            smooth = [smooth_of(n, b) for b in range(S)]
            layer = []
            for a in range(S):
                value = -1.0 / compress
                for b in range(S):
                    factor = 0.5 * (chi_ref[a, b] + chi_ref[b, a]) + 1.0 / compress
                    value = value + factor * smooth[b]
                layer.append(value)
            layers.append(layer)
        for a in range(S):
            for z in range(CZ):
                value = layers[z + 1][a]
                own = value[1:-1]
                potential_ref[a, z] = own
                force_ref[0, a, z] = (layers[z][a][1:-1] - layers[z + 2][a][1:-1]) * 0.5
                force_ref[1, a, z] = (value[:-2] - value[2:]) * 0.5
                force_ref[2, a, z] = (pltpu.roll(own, 1, 1) - pltpu.roll(own, Y - 1, 1)) * 0.5


def gathered(block):
    slab_count = lax.axis_size("slab")
    if slab_count > 8:
        block = lax.all_gather(block, "slab")
    else:
        turned = [
            lax.ppermute(block, "slab", [(i, (i + k) % slab_count) for i in range(slab_count)])
            for k in range(1, slab_count)
        ]
        block = jnp.stack([block] + turned)
    for axis in ("beads", "sub"):
        count = lax.axis_size(axis)
        turned = [
            lax.ppermute(block, axis, [(i, (i + k) % count) for i in range(count)])
            for k in range(1, count)
        ]
        block = jnp.concatenate([block] + turned)
    return block


def on_device(dest_slab, local_cell, species, bead_mass, rise_fraction, chi_matrix):
    bead_count = local_cell.shape[0]
    slab_count = lax.axis_size("slab")
    group_count = lax.axis_size(("beads", "sub"))
    heights = slab_count * CZ
    own_rows = X // group_count
    scale = CZ * X * Y / (bead_count * group_count)
    lines = bead_count // 128
    chunks = bead_count // CHUNK
    vmem = pl.BlockSpec(memory_space=pltpu.VMEM)
    smem = pl.BlockSpec(memory_space=pltpu.SMEM)
    block = pl.pallas_call(
        functools.partial(sort_kernel, heights, scale),
        out_shape=jax.ShapeDtypeStruct((3 * chunks + 8, CHUNK), jnp.float32),
        in_specs=[vmem] * 5,
        out_specs=vmem,
        scratch_shapes=[
            pltpu.VMEM((9 * chunks, bead_count), jnp.bfloat16),
            pltpu.VMEM((CHUNK, bead_count), jnp.bfloat16),
        ],
        compiler_params=pltpu.CompilerParams(vmem_limit_bytes=32 << 20),
        name="sort_beads",
    )(*[x.reshape(lines, 128) for x in (dest_slab, local_cell, species, bead_mass, rise_fraction)])
    lists = gathered(block)
    place = jnp.stack([lax.axis_index("slab"), lax.axis_index(("beads", "sub"))]).astype(jnp.int32)
    list_lines = 3 * chunks + 8
    windows = -(-(own_rows // BUCKET + 1) // WINDOW_BUCKETS)
    potential, force = pl.pallas_call(
        functools.partial(grid_kernel, heights, own_rows),
        grid=(lists.shape[0] // BLOCK_LISTS,),
        out_shape=(
            jax.ShapeDtypeStruct((S, CZ, own_rows, Y), jnp.float32),
            jax.ShapeDtypeStruct((3, S, CZ, own_rows, Y), jnp.float32),
        ),
        in_specs=[
            smem,
            smem,
            pl.BlockSpec((BLOCK_LISTS, list_lines, CHUNK), lambda i: (i, 0, 0)),
        ],
        out_specs=(
            pl.BlockSpec((S, CZ, own_rows, Y), lambda i: (0, 0, 0, 0)),
            pl.BlockSpec((3, S, CZ, own_rows, Y), lambda i: (0, 0, 0, 0, 0)),
        ),
        scratch_shapes=[
            pltpu.VMEM((BLOCK_LISTS * chunks, CHUNK), jnp.int32),
            pltpu.VMEM((BLOCK_LISTS * chunks, CHUNK), jnp.int32),
            pltpu.VMEM((2 * (CZ + 2), BLOCK_LISTS * chunks, CHUNK), jnp.float32),
            pltpu.VMEM((BLOCK_LISTS, 128), jnp.int32),
            pltpu.SMEM((BLOCK_LISTS, 128), jnp.int32),
            pltpu.VMEM((CZ + 2, 2, max(windows * WINDOW, own_rows + 2 * RIM), 2 * Y), jnp.float32),
            pltpu.SemaphoreType.DMA,
        ],
        compiler_params=pltpu.CompilerParams(vmem_limit_bytes=48 << 20),
        name="grid_fields",
    )(chi_matrix, place, lists)
    return (potential, force)


def solution(mesh):
    placed = (
        P(("runs", "slab", "beads", "sub"), None),
        P(("runs", "slab", "beads", "sub")),
        P(("runs", "slab", "beads", "sub")),
        P(("runs", "slab", "beads", "sub")),
        P(("runs", "slab", "beads", "sub")),
        P(),
    )
    return jax.shard_map(
        on_device,
        mesh=mesh,
        in_specs=placed,
        out_specs=(
            P("runs", "slab", ("beads", "sub"), None),
            P(None, "runs", "slab", ("beads", "sub"), None),
        ),
        check_vma=False,
    )
```

```python
import functools

import jax
import jax.numpy as jnp
from jax import lax
from jax.experimental import pallas as pl
from jax.experimental.pallas import tpu as pltpu
from jax.sharding import PartitionSpec as P

S = 4
X = 256
Y = 128
CZ = 2

compress = 0.5

BUCKET = 8
BUCKETS = X // BUCKET
RIM = 4
LINE = 128
WINDOW = 2 * BUCKET
TARGETS = CZ + 2
META = 8
GROUP = 4

NT = (((1,), (1,)), ((), ()))


def pieces_of(values):
    parts = []
    for _ in range(2):
        part = values.astype(jnp.bfloat16)
        parts.append(part)
        values = values - part.astype(jnp.float32)
    parts.append(values.astype(jnp.bfloat16))
    return parts


def sort_kernel(key_ref, lower_ref, upper_ref, out_ref, left_ref, right_ref):
    lines = key_ref.shape[0]
    places = lines * LINE
    halves = lines // 2
    key = key_ref[...]
    row = (key // Y) & (X - 1)
    bucket = ((row + RIM) & (X - 1)) // BUCKET
    member_iota = lax.broadcasted_iota(jnp.int32, (BUCKETS, LINE), 0)
    members = [
        jnp.where(bucket[i : i + 1, :] == member_iota, 1.0, 0.0) for i in range(lines)
    ]
    stacked = jnp.concatenate([m.astype(jnp.bfloat16) for m in members], 0)
    source = lax.broadcasted_iota(jnp.int32, (LINE, 2 * LINE), 0)
    target = lax.broadcasted_iota(jnp.int32, (LINE, 2 * LINE), 1)
    before = jnp.where(source < target, 1.0, 0.0).astype(jnp.bfloat16)
    counted = jnp.dot(stacked, before, preferred_element_type=jnp.float32)
    total = jnp.zeros((BUCKETS, LINE), jnp.float32)
    ranks = []
    for i in range(lines):
        ranks.append(counted[i * BUCKETS : (i + 1) * BUCKETS, :LINE] + total)
        total = total + counted[i * BUCKETS : (i + 1) * BUCKETS, LINE:]
    start = total
    shift = 1
    while shift < BUCKETS:
        start = start + jnp.where(member_iota >= shift, pltpu.roll(start, shift, 0), 0.0)
        shift *= 2
    start = start - total
    lane = lax.broadcasted_iota(jnp.int32, (BUCKETS, LINE), 1)
    starts = jnp.sum(jnp.where(member_iota == lane, start, 0.0), 0, keepdims=True)
    starts = jnp.where(lane[:1] < BUCKETS, starts, float(places))
    lower, upper = lower_ref[...], upper_ref[...]
    parts = [part.astype(jnp.float32) for part in (key // 65536, (key // 256) & 255, key & 255)]
    parts += [part.astype(jnp.float32) for part in pieces_of(lower) + pieces_of(upper)]
    half_iota = lax.broadcasted_iota(jnp.int32, (halves, LINE), 0)
    slot_iota = lax.broadcasted_iota(jnp.int32, (2 * LINE, LINE), 0)
    for i in range(lines):
        place = jnp.sum(members[i] * (ranks[i] + start), 0, keepdims=True).astype(jnp.int32)
        hit = half_iota == place // (2 * LINE)
        for n, part in enumerate(parts):
            left_ref[n * halves : (n + 1) * halves, i * LINE : (i + 1) * LINE] = jnp.where(
                hit, part[i : i + 1, :], 0.0
            ).astype(jnp.bfloat16)
        right_ref[:, i * LINE : (i + 1) * LINE] = jnp.where(
            slot_iota == (place & (2 * LINE - 1)), 1.0, 0.0
        ).astype(jnp.bfloat16)
    placed = lax.dot_general(
        left_ref[...], right_ref[...], NT, preferred_element_type=jnp.float32
    )

    def part_of(n):
        return placed[n * halves : (n + 1) * halves]

    sorted_values = (
        part_of(0) * 65536.0 + part_of(1) * 256.0 + part_of(2),
        part_of(3) + part_of(4) + part_of(5),
        part_of(6) + part_of(7) + part_of(8),
    )
    for n, value in enumerate(sorted_values):
        out_ref[n * lines : n * lines + halves] = value[:, :LINE]
        out_ref[n * lines + halves : (n + 1) * lines] = value[:, LINE:]
    out_ref[3 * lines : 3 * lines + META] = jnp.broadcast_to(starts, (META, LINE))


def shares_of(lower, upper, height, first, heights):
    shares = (
        0.0625 * lower,
        0.25 * lower + 0.0625 * upper,
        0.375 * lower + 0.25 * upper,
        0.25 * lower + 0.375 * upper,
        0.0625 * lower + 0.25 * upper,
        0.0625 * upper,
    )
    none = jnp.zeros_like(lower)
    if heights == 8:
        turn = (first + 2 + heights - height) & 7
        kept = list(shares) + [none, none]
        for bit, length in ((4, 7), (2, 5), (1, 4)):
            chosen = (turn & bit) != 0
            kept = [
                jnp.where(chosen, kept[(i + bit) % 8], kept[i]) for i in range(length)
            ]
        return kept
    amounts = []
    for n in range(TARGETS):
        above = (first + n + 2 + heights - height) % heights
        amount = none
        for d, share in enumerate(shares):
            amount = jnp.where(above == d, share, amount)
        amounts.append(amount)
    return amounts


def spare_lines(lists):
    return max(2, lists // 4)


def deposit(heights, own_rows, slab, group, lists_ref, first_list, lists, grid_ref, scratch):
    near_ref, column_ref, amount_ref, starts_ref, starts_smem, sem = scratch
    lines = (lists_ref.shape[1] - META) // 3
    places = lines * LINE
    halves = lines // 2
    buckets = own_rows // BUCKET + 1
    windows = -(-buckets // 2)

    starts_ref[0:lists] = lists_ref[first_list : first_list + lists, 3 * lines, :].astype(jnp.int32)
    copy = pltpu.make_async_copy(starts_ref, starts_smem, sem)
    copy.start()
    first_row = group * own_rows - RIM

    def spread(i, carry):
        key = lists_ref[first_list + i, 0:lines, :].astype(jnp.int32)
        lower = lists_ref[first_list + i, lines : 2 * lines, :]
        upper = lists_ref[first_list + i, 2 * lines : 3 * lines, :]
        spot = pl.ds(pl.multiple_of(i * lines, lines), lines)
        plane = key // (X * Y)
        species = plane // heights
        height = plane - species * heights
        row = (key // Y) & (X - 1)
        near_ref[spot, :] = ((row - first_row) & (X - 1)) + (species // 2) * 1024
        column_ref[spot, :] = ((key & (Y - 1)) + (species & 1) * Y).astype(jnp.float32)
        for n, amount in enumerate(shares_of(lower, upper, height, slab * CZ - 1, heights)):
            high = amount.astype(jnp.bfloat16).astype(jnp.float32)
            amount_ref[2 * n, spot, :] = high
            amount_ref[2 * n + 1, spot, :] = amount - high
        return carry

    lax.fori_loop(0, lists, spread, 0, unroll=2)
    copy.wait()

    near_iota = lax.broadcasted_iota(jnp.int32, (2 * WINDOW, LINE), 0)
    near_iota = jnp.where(near_iota >= WINDOW, near_iota + (1024 - WINDOW), near_iota)
    column_iota = lax.broadcasted_iota(jnp.int32, (2 * Y, LINE), 0).astype(jnp.float32).astype(jnp.bfloat16)
    one, zero = jnp.bfloat16(1), jnp.bfloat16(0)

    def operands_of(i, line, base):
        at = pl.ds(i * lines + (line & 1) * halves + ((line & (lines - 1)) >> 1), 1)
        hit = jnp.where(near_ref[at, :] - base == near_iota, 1.0, 0.0).astype(jnp.bfloat16)
        left = [
            hit * jnp.broadcast_to(amount_ref[n, at, :], hit.shape).astype(jnp.bfloat16)
            for n in range(2 * TARGETS)
        ]
        column = jnp.broadcast_to(column_ref[at, :], (2 * Y, LINE)).astype(jnp.bfloat16)
        return jnp.concatenate(left, 0), jnp.where(column == column_iota, one, zero)

    def add_product(window, entries):
        got = 0.0
        for g in range(0, len(entries), GROUP):
            pairs = [operands_of(*entry) for entry in entries[g : g + GROUP]]
            got = got + lax.dot_general(
                jnp.concatenate([pair[0] for pair in pairs], 1),
                jnp.concatenate([pair[1] for pair in pairs], 1),
                NT,
                preferred_element_type=jnp.float32,
            )
        for n in range(TARGETS):
            for half in range(2):
                high = (2 * n * 2 + half) * WINDOW
                low = ((2 * n + 1) * 2 + half) * WINDOW
                rows = slice(window * WINDOW, (window + 1) * WINDOW)
                grid_ref[n, half, rows, :] += got[high : high + WINDOW] + got[low : low + WINDOW]

    never = 8192
    spare = spare_lines(lists)

    def range_of(window):
        usual = min(2, buckets - 2 * window) + 1
        low = group * (own_rows // BUCKET) + 2 * window
        high = low + usual - 1
        wrapped = jnp.where(high > BUCKETS, BUCKETS, 0)
        lead = jnp.where(high > BUCKETS, places, 0)

        def span_of(i):
            begin = starts_smem[i, low]
            end = starts_smem[i, high - wrapped] + lead
            first = begin // LINE
            count = jnp.where(end > begin, (end + (LINE - 1)) // LINE - first, 0)
            return first, jnp.minimum(count, lines)

        return usual, span_of

    flags = []
    for window in range(windows):
        usual, span_of = range_of(window)
        base = window * WINDOW
        spare_list = [jnp.int32(0)] * spare
        spare_line = [jnp.int32(0)] * spare
        spare_base = [jnp.int32(never)] * spare
        used = jnp.int32(0)
        most = jnp.int32(0)
        entries = []
        for i in range(lists):
            first, count = span_of(i)
            for t in range(usual):
                entries.append((i, first + t, jnp.where(t < count, base, never)))
            over = count > usual
            for k in range(spare):
                mine = over & (used == k)
                spare_list[k] = jnp.where(mine, i, spare_list[k])
                spare_line[k] = jnp.where(mine, first + usual, spare_line[k])
                spare_base[k] = jnp.where(mine, base, spare_base[k])
            used = used + jnp.where(over, 1, 0)
            most = jnp.maximum(most, count)
        for k in range(spare):
            entries.append((spare_list[k], spare_line[k], spare_base[k]))
        add_product(window, entries)
        flags.append((used > spare) | (most > usual + 1))

    def rest_of_window(window):
        usual, span_of = range_of(window)
        base = window * WINDOW

        def rest_of(i, before):
            first, count = span_of(i)
            over = count > usual
            done = usual + jnp.where(over & (before < spare), 1, 0)

            def four_lines(turn, carry):
                ahead = [done + turn * 4 + k for k in range(4)]
                add_product(window, [(i, first + t, jnp.where(t < count, base, never)) for t in ahead])
                return carry

            lax.fori_loop(0, (count - done + 3) // 4, four_lines, 0)
            return before + jnp.where(over, 1, 0)

        lax.fori_loop(0, lists, rest_of, jnp.int32(0))

    @pl.when(functools.reduce(jnp.logical_or, flags))
    def _():
        for window in range(windows):
            pl.when(flags[window])(functools.partial(rest_of_window, window))


def fields(own_rows, chi_ref, grid_ref, potential_ref, force_ref):
    rows = own_rows + 2

    def smooth_of(n, b):
        lanes = slice((b % 2) * Y, (b % 2 + 1) * Y)

        def shifted(k):
            return grid_ref[n, b // 2, RIM - 3 + k : RIM - 3 + k + rows, lanes]

        value = (
            0.375 * shifted(2) + 0.25 * (shifted(1) + shifted(3)) + 0.0625 * (shifted(0) + shifted(4))
        )
        close = pltpu.roll(value, 1, 1) + pltpu.roll(value, Y - 1, 1)
        far = pltpu.roll(value, 2, 1) + pltpu.roll(value, Y - 2, 1)
        return 0.375 * value + 0.25 * close + 0.0625 * far

    layers = []
    for n in range(TARGETS):
        smooth = [smooth_of(n, b) for b in range(S)]
        layer = []
        for a in range(S):
            value = -1.0 / compress
            for b in range(S):
                factor = 0.5 * (chi_ref[a, b] + chi_ref[b, a]) + 1.0 / compress
                value = value + factor * smooth[b]
            layer.append(value)
        layers.append(layer)
    for a in range(S):
        for z in range(CZ):
            value = layers[z + 1][a]
            own = value[1:-1]
            potential_ref[a, z] = own
            force_ref[0, a, z] = (layers[z][a][1:-1] - layers[z + 2][a][1:-1]) * 0.5
            force_ref[1, a, z] = (value[:-2] - value[2:]) * 0.5
            force_ref[2, a, z] = (pltpu.roll(own, 1, 1) - pltpu.roll(own, Y - 1, 1)) * 0.5


def grid_kernel(heights, own_rows, lists, chi_ref, place_ref, lists_ref, potential_ref, force_ref, grid_ref, *scratch):
    step = pl.program_id(0)

    @pl.when(step == 0)
    def _():
        grid_ref[...] = jnp.zeros_like(grid_ref)

    deposit(heights, own_rows, place_ref[0], place_ref[1], lists_ref, 0, lists, grid_ref, scratch)

    @pl.when(step == pl.num_programs(0) - 1)
    def _():
        fields(own_rows, chi_ref, grid_ref, potential_ref, force_ref)


def deposit_scratch(lists, lines):
    return [
        pltpu.VMEM((lists * lines, LINE), jnp.int32),
        pltpu.VMEM((lists * lines, LINE), jnp.float32),
        pltpu.VMEM((2 * TARGETS, lists * lines, LINE), jnp.float32),
        pltpu.VMEM((max(lists, 8), LINE), jnp.int32),
        pltpu.SMEM((max(lists, 8), LINE), jnp.int32),
        pltpu.SemaphoreType.DMA,
    ]


def gathered(block):
    slab_count = lax.axis_size("slab")
    if slab_count > 8:
        block = lax.all_gather(block, "slab")
    else:
        turned = [
            lax.ppermute(block, "slab", [(i, (i + k) % slab_count) for i in range(slab_count)])
            for k in range(1, slab_count)
        ]
        block = jnp.stack([block] + turned)
    for axis in ("beads", "sub"):
        count = lax.axis_size(axis)
        turned = [
            lax.ppermute(block, axis, [(i, (i + k) % count) for i in range(count)])
            for k in range(1, count)
        ]
        block = jnp.concatenate([block] + turned)
    return block


def on_device(dest_slab, local_cell, species, bead_mass, rise_fraction, chi_matrix):
    bead_count = local_cell.shape[0]
    slab_count = lax.axis_size("slab")
    group_count = lax.axis_size(("beads", "sub"))
    heights = slab_count * CZ
    own_rows = X // group_count
    scale = CZ * X * Y / (bead_count * group_count)
    lines = bead_count // LINE
    list_lines = 3 * lines + META
    dest, cell, kind, mass, rise = (
        x.reshape(lines, LINE) for x in (dest_slab, local_cell, species, bead_mass, rise_fraction)
    )
    height = dest * CZ + cell // (X * Y)
    key = (kind * heights + height) * (X * Y) + (cell & (X * Y - 1))
    lower = mass * scale * (1.0 - rise)
    upper = mass * scale * rise
    vmem = pl.BlockSpec(memory_space=pltpu.VMEM)
    smem = pl.BlockSpec(memory_space=pltpu.SMEM)
    block = pl.pallas_call(
        sort_kernel,
        out_shape=jax.ShapeDtypeStruct((list_lines, LINE), jnp.float32),
        in_specs=[vmem] * 3,
        out_specs=vmem,
        scratch_shapes=[
            pltpu.VMEM((9 * lines // 2, bead_count), jnp.bfloat16),
            pltpu.VMEM((2 * LINE, bead_count), jnp.bfloat16),
        ],
        compiler_params=pltpu.CompilerParams(vmem_limit_bytes=32 << 20),
        name="sort_beads",
    )(key, lower, upper)
    lists = gathered(block)
    place = jnp.stack([lax.axis_index("slab"), lax.axis_index(("beads", "sub"))]).astype(jnp.int32)
    together = 16
    windows = -(-(own_rows // BUCKET + 1) // 2)
    potential, force = pl.pallas_call(
        functools.partial(grid_kernel, heights, own_rows, together),
        grid=(lists.shape[0] // together,),
        out_shape=(
            jax.ShapeDtypeStruct((S, CZ, own_rows, Y), jnp.float32),
            jax.ShapeDtypeStruct((3, S, CZ, own_rows, Y), jnp.float32),
        ),
        in_specs=[
            smem,
            smem,
            pl.BlockSpec((together, list_lines, LINE), lambda i: (i, 0, 0)),
        ],
        out_specs=(
            pl.BlockSpec((S, CZ, own_rows, Y), lambda i: (0, 0, 0, 0)),
            pl.BlockSpec((3, S, CZ, own_rows, Y), lambda i: (0, 0, 0, 0, 0)),
        ),
        scratch_shapes=[
            pltpu.VMEM((TARGETS, 2, windows * WINDOW, 2 * Y), jnp.float32),
        ]
        + deposit_scratch(together, lines),
        compiler_params=pltpu.CompilerParams(vmem_limit_bytes=48 << 20),
        name="grid_fields",
    )(chi_matrix, place, lists)
    return (potential, force)


def solution(mesh):
    placed = (
        P(("runs", "slab", "beads", "sub"), None),
        P(("runs", "slab", "beads", "sub")),
        P(("runs", "slab", "beads", "sub")),
        P(("runs", "slab", "beads", "sub")),
        P(("runs", "slab", "beads", "sub")),
        P(),
    )
    return jax.shard_map(
        on_device,
        mesh=mesh,
        in_specs=placed,
        out_specs=(
            P("runs", "slab", ("beads", "sub"), None),
            P(None, "runs", "slab", ("beads", "sub"), None),
        ),
        check_vma=False,
    )
```

```python
import functools

import jax
import jax.numpy as jnp
from jax import lax
from jax.experimental import pallas as pl
from jax.experimental.pallas import tpu as pltpu
from jax.sharding import PartitionSpec as P

S = 4
X = 256
Y = 128
CZ = 2

compress = 0.5

BUCKET = 8
BUCKETS = X // BUCKET
RIM = 4
LINE = 128
WINDOW = 2 * BUCKET
TARGETS = CZ + 2
META = 8
GROUP = 4
SORT_GROUP = 2

NT = (((1,), (1,)), ((), ()))


def pieces_of(values):
    parts = []
    for _ in range(2):
        part = values.astype(jnp.bfloat16)
        parts.append(part)
        values = values - part.astype(jnp.float32)
    parts.append(values.astype(jnp.bfloat16))
    return parts


def sort_kernel(heights, scale, *refs):
    sources, out_ref, targets, sems = refs[:5], refs[5], refs[6:11], refs[11]
    copies = [
        pltpu.make_async_copy(source, target, sems.at[i])
        for i, (source, target) in enumerate(zip(sources, targets))
    ]
    for copy in copies:
        copy.start()
    dest_ref, cell_ref, species_ref, mass_ref, rise_ref = targets
    lines = cell_ref.shape[0]
    places = lines * LINE
    halves = lines // 2
    copies[1].wait()
    cell = cell_ref[...]
    row = (cell // Y) & (X - 1)
    bucket = ((row + RIM) & (X - 1)) // BUCKET
    member_iota = lax.broadcasted_iota(jnp.int32, (BUCKETS, LINE), 0)
    members = [
        jnp.where(bucket[i : i + 1, :] == member_iota, 1.0, 0.0) for i in range(lines)
    ]
    stacked = jnp.concatenate([m.astype(jnp.bfloat16) for m in members], 0)
    source = lax.broadcasted_iota(jnp.int32, (LINE, 2 * LINE), 0)
    target = lax.broadcasted_iota(jnp.int32, (LINE, 2 * LINE), 1)
    before = jnp.where(source < target, 1.0, 0.0).astype(jnp.bfloat16)
    counted = jnp.dot(stacked, before, preferred_element_type=jnp.float32)
    total = jnp.zeros((BUCKETS, LINE), jnp.float32)
    ranks = []
    for i in range(lines):
        ranks.append(counted[i * BUCKETS : (i + 1) * BUCKETS, :LINE] + total)
        total = total + counted[i * BUCKETS : (i + 1) * BUCKETS, LINE:]
    start = total
    shift = 1
    while shift < BUCKETS:
        start = start + jnp.where(member_iota >= shift, pltpu.roll(start, shift, 0), 0.0)
        shift *= 2
    start = start - total
    lane = lax.broadcasted_iota(jnp.int32, (BUCKETS, LINE), 1)
    starts = jnp.sum(jnp.where(member_iota == lane, start, 0.0), 0, keepdims=True)
    starts = jnp.where(lane[:1] < BUCKETS, starts, float(places))
    for i in (0, 2, 3, 4):
        copies[i].wait()
    height = dest_ref[...] * CZ + cell // (X * Y)
    key = (species_ref[...] * heights + height) * (X * Y) + (cell & (X * Y - 1))
    mass = mass_ref[...] * scale
    lower = mass * (1.0 - rise_ref[...])
    upper = mass * rise_ref[...]
    parts = [part.astype(jnp.float32) for part in (key // 65536, (key // 256) & 255, key & 255)]
    parts += [part.astype(jnp.float32) for part in pieces_of(lower) + pieces_of(upper)]
    half_iota = lax.broadcasted_iota(jnp.int32, (halves, LINE), 0)
    slot_iota = lax.broadcasted_iota(jnp.int32, (2 * LINE, LINE), 0)
    placed = 0.0
    for first in range(0, lines, SORT_GROUP):
        lefts, rights = [], []
        for i in range(first, first + SORT_GROUP):
            place = jnp.sum(members[i] * (ranks[i] + start), 0, keepdims=True).astype(jnp.int32)
            hit = half_iota == place // (2 * LINE)
            lefts.append(
                jnp.concatenate([jnp.where(hit, part[i : i + 1, :], 0.0) for part in parts], 0)
            )
            rights.append(jnp.where(slot_iota == (place & (2 * LINE - 1)), 1.0, 0.0))
        placed = placed + lax.dot_general(
            jnp.concatenate(lefts, 1).astype(jnp.bfloat16),
            jnp.concatenate(rights, 1).astype(jnp.bfloat16),
            NT,
            preferred_element_type=jnp.float32,
        )

    def part_of(n):
        return placed[n * halves : (n + 1) * halves]

    sorted_values = (
        part_of(0) * 65536.0 + part_of(1) * 256.0 + part_of(2),
        part_of(3) + part_of(4) + part_of(5),
        part_of(6) + part_of(7) + part_of(8),
    )
    for n, value in enumerate(sorted_values):
        out_ref[n * lines : n * lines + halves] = value[:, :LINE]
        out_ref[n * lines + halves : (n + 1) * lines] = value[:, LINE:]
    out_ref[3 * lines : 3 * lines + META] = jnp.broadcast_to(starts, (META, LINE))


def shares_of(lower, upper, height, first, heights):
    shares = (
        0.0625 * lower,
        0.25 * lower + 0.0625 * upper,
        0.375 * lower + 0.25 * upper,
        0.25 * lower + 0.375 * upper,
        0.0625 * lower + 0.25 * upper,
        0.0625 * upper,
    )
    none = jnp.zeros_like(lower)
    if heights == 8:
        turn = (first + 2 + heights - height) & 7
        kept = list(shares) + [none, none]
        for bit, length in ((4, 7), (2, 5), (1, 4)):
            chosen = (turn & bit) != 0
            kept = [
                jnp.where(chosen, kept[(i + bit) % 8], kept[i]) for i in range(length)
            ]
        return kept
    amounts = []
    for n in range(TARGETS):
        above = (first + n + 2 + heights - height) % heights
        amount = none
        for d, share in enumerate(shares):
            amount = jnp.where(above == d, share, amount)
        amounts.append(amount)
    return amounts


def spare_lines(lists):
    return max(2, lists // 4)


def deposit(heights, own_rows, slab, group, lists_ref, before_ref, grid_ref, scratch):
    near_ref, column_ref, amount_ref, starts_ref, starts_smem, sem = scratch
    lists = lists_ref.shape[0]
    lines = (lists_ref.shape[1] - META) // 3
    places = lines * LINE
    halves = lines // 2
    buckets = own_rows // BUCKET + 1
    windows = -(-buckets // 2)

    starts_ref[0:lists] = lists_ref[:, 3 * lines, :].astype(jnp.int32)
    copy = pltpu.make_async_copy(starts_ref, starts_smem, sem)
    copy.start()
    first_row = group * own_rows - RIM

    def spread(i, carry):
        key = lists_ref[i, 0:lines, :].astype(jnp.int32)
        lower = lists_ref[i, lines : 2 * lines, :]
        upper = lists_ref[i, 2 * lines : 3 * lines, :]
        spot = pl.ds(pl.multiple_of(i * lines, lines), lines)
        plane = key // (X * Y)
        species = plane // heights
        height = plane - species * heights
        row = (key // Y) & (X - 1)
        near_ref[spot, :] = ((row - first_row) & (X - 1)) + (species // 2) * 1024
        column_ref[spot, :] = ((key & (Y - 1)) + (species & 1) * Y).astype(jnp.float32)
        for n, amount in enumerate(shares_of(lower, upper, height, slab * CZ - 1, heights)):
            high = amount.astype(jnp.bfloat16).astype(jnp.float32)
            amount_ref[2 * n, spot, :] = high
            amount_ref[2 * n + 1, spot, :] = amount - high
        return carry

    lax.fori_loop(0, lists, spread, 0, unroll=2)
    copy.wait()

    near_iota = lax.broadcasted_iota(jnp.int32, (2 * WINDOW, LINE), 0)
    near_iota = jnp.where(near_iota >= WINDOW, near_iota + (1024 - WINDOW), near_iota)
    column_iota = lax.broadcasted_iota(jnp.int32, (2 * Y, LINE), 0).astype(jnp.float32).astype(jnp.bfloat16)
    one, zero = jnp.bfloat16(1), jnp.bfloat16(0)

    def operands_of(i, line, base):
        at = pl.ds(i * lines + (line & 1) * halves + ((line & (lines - 1)) >> 1), 1)
        hit = jnp.where(near_ref[at, :] - base == near_iota, 1.0, 0.0).astype(jnp.bfloat16)
        left = [
            hit * jnp.broadcast_to(amount_ref[n, at, :], hit.shape).astype(jnp.bfloat16)
            for n in range(2 * TARGETS)
        ]
        column = jnp.broadcast_to(column_ref[at, :], (2 * Y, LINE)).astype(jnp.bfloat16)
        return jnp.concatenate(left, 0), jnp.where(column == column_iota, one, zero)

    def add_product(window, entries, base_ref):
        got = 0.0
        for g in range(0, len(entries), GROUP):
            pairs = [operands_of(*entry) for entry in entries[g : g + GROUP]]
            got = got + lax.dot_general(
                jnp.concatenate([pair[0] for pair in pairs], 1),
                jnp.concatenate([pair[1] for pair in pairs], 1),
                NT,
                preferred_element_type=jnp.float32,
            )
        for n in range(TARGETS):
            for half in range(2):
                high = (2 * n * 2 + half) * WINDOW
                low = ((2 * n + 1) * 2 + half) * WINDOW
                rows = slice(window * WINDOW, (window + 1) * WINDOW)
                value = got[high : high + WINDOW] + got[low : low + WINDOW]
                if base_ref is not None:
                    value = value + base_ref[n, half, rows, :]
                grid_ref[n, half, rows, :] = value

    never = 8192
    spare = spare_lines(lists)

    def range_of(window):
        usual = min(2, buckets - 2 * window) + 1
        low = group * (own_rows // BUCKET) + 2 * window
        high = low + usual - 1
        wrapped = jnp.where(high > BUCKETS, BUCKETS, 0)
        lead = jnp.where(high > BUCKETS, places, 0)

        def span_of(i):
            begin = starts_smem[i, low]
            end = starts_smem[i, high - wrapped] + lead
            first = begin // LINE
            count = jnp.where(end > begin, (end + (LINE - 1)) // LINE - first, 0)
            return first, jnp.minimum(count, lines)

        return usual, span_of

    flags = []
    for window in range(windows):
        usual, span_of = range_of(window)
        base = window * WINDOW
        spare_list = [jnp.int32(0)] * spare
        spare_line = [jnp.int32(0)] * spare
        spare_base = [jnp.int32(never)] * spare
        used = jnp.int32(0)
        most = jnp.int32(0)
        entries = []
        for i in range(lists):
            first, count = span_of(i)
            for t in range(usual):
                entries.append((i, first + t, jnp.where(t < count, base, never)))
            over = count > usual
            for k in range(spare):
                mine = over & (used == k)
                spare_list[k] = jnp.where(mine, i, spare_list[k])
                spare_line[k] = jnp.where(mine, first + usual, spare_line[k])
                spare_base[k] = jnp.where(mine, base, spare_base[k])
            used = used + jnp.where(over, 1, 0)
            most = jnp.maximum(most, count)
        for k in range(spare):
            entries.append((spare_list[k], spare_line[k], spare_base[k]))
        add_product(window, entries, before_ref)
        flags.append((used > spare) | (most > usual + 1))

    def rest_of_window(window):
        usual, span_of = range_of(window)
        base = window * WINDOW

        def rest_of(i, before):
            first, count = span_of(i)
            over = count > usual
            done = usual + jnp.where(over & (before < spare), 1, 0)

            def four_lines(turn, carry):
                ahead = [done + turn * 4 + k for k in range(4)]
                entries = [(i, first + t, jnp.where(t < count, base, never)) for t in ahead]
                add_product(window, entries, grid_ref)
                return carry

            lax.fori_loop(0, (count - done + 3) // 4, four_lines, 0)
            return before + jnp.where(over, 1, 0)

        lax.fori_loop(0, lists, rest_of, jnp.int32(0))

    @pl.when(functools.reduce(jnp.logical_or, flags))
    def _():
        for window in range(windows):
            pl.when(flags[window])(functools.partial(rest_of_window, window))


def fields(
    own_rows, chi_ref, grid_ref, potential_ref, force_ref, potential_hbm, force_hbm, sems
):
    rows = own_rows + 2

    def smooth_of(n, b):
        lanes = slice((b % 2) * Y, (b % 2 + 1) * Y)

        def shifted(k):
            return grid_ref[n, b // 2, RIM - 3 + k : RIM - 3 + k + rows, lanes]

        value = (
            0.375 * shifted(2) + 0.25 * (shifted(1) + shifted(3)) + 0.0625 * (shifted(0) + shifted(4))
        )
        close = pltpu.roll(value, 1, 1) + pltpu.roll(value, Y - 1, 1)
        far = pltpu.roll(value, 2, 1) + pltpu.roll(value, Y - 2, 1)
        return 0.375 * value + 0.25 * close + 0.0625 * far

    factors = [
        [0.5 * (chi_ref[a, b] + chi_ref[b, a]) + 1.0 / compress for b in range(S)] for a in range(S)
    ]
    smooth = [[smooth_of(n, b) for b in range(S)] for n in range(TARGETS)]
    copies = []
    for a in range(S):
        layers = []
        for n in range(TARGETS):
            value = -1.0 / compress
            for b in range(S):
                value = value + factors[a][b] * smooth[n][b]
            layers.append(value)
        for z in range(CZ):
            value = layers[z + 1]
            own = value[1:-1]
            potential_ref[a, z] = own
            force_ref[0, a, z] = (layers[z][1:-1] - layers[z + 2][1:-1]) * 0.5
            force_ref[1, a, z] = (value[:-2] - value[2:]) * 0.5
            force_ref[2, a, z] = (pltpu.roll(own, 1, 1) - pltpu.roll(own, Y - 1, 1)) * 0.5
            at = 1 + 2 * (a * CZ + z)
            copies += [
                pltpu.make_async_copy(potential_ref.at[a, z], potential_hbm.at[a, z], sems.at[at]),
                pltpu.make_async_copy(force_ref.at[:, a, z], force_hbm.at[:, a, z], sems.at[at + 1]),
            ]
            copies[-2].start()
            copies[-1].start()
    for copy in copies:
        copy.wait()


def part_kernel(heights, own_rows, role, *refs):
    step = pl.program_id(0) if role.steps > 1 else 0
    refs = list(refs)
    chi_hbm = refs.pop(0) if role.last else None
    lists_ref = refs.pop(0)
    before_ref = None if role.first else refs.pop(0)
    if role.last:
        potential_ref, force_ref = refs.pop(0), refs.pop(0)
    grid_ref = refs.pop(0)
    if role.last:
        chi_ref, potential_vmem, force_vmem, sems = refs[:4]
        del refs[:4]
        chi_copy = pltpu.make_async_copy(chi_hbm, chi_ref, sems.at[0])
        pl.when(step == 0)(chi_copy.start)

    if role.steps > 1:

        @pl.when(step == 0)
        def _():
            grid_ref[...] = jnp.zeros_like(grid_ref) if role.first else before_ref[...]

        before_ref = grid_ref

    deposit(heights, own_rows, lax.axis_index("slab"), lax.axis_index(("beads", "sub")), lists_ref, before_ref, grid_ref, refs)

    if role.last:

        @pl.when(step == role.steps - 1)
        def _():
            chi_copy.wait()
            fields(
                own_rows, chi_ref, grid_ref, potential_vmem, force_vmem, potential_ref, force_ref, sems
            )


class Role:
    def __init__(self, first, last, steps):
        self.first, self.last, self.steps = first, last, steps


def deposit_call(heights, own_rows, lists, before, chi):
    total, list_lines, _ = lists.shape
    lines = (list_lines - META) // 3
    together = min(8, total)
    role = Role(before is None, chi is not None, total // together)
    whole = pl.BlockSpec(memory_space=pltpu.VMEM)
    hbm = pl.BlockSpec(memory_space=pl.ANY)
    windows = -(-(own_rows // BUCKET + 1) // 2)
    grid_shape = (TARGETS, 2, windows * WINDOW, 2 * Y)
    operands, specs = [], []
    if role.last:
        operands.append(pltpu.with_memory_space_constraint(chi, pltpu.MemorySpace.HBM))
        specs.append(hbm)
    operands.append(lists)
    specs.append(
        whole if role.steps == 1 else pl.BlockSpec((together, list_lines, LINE), lambda i: (i, 0, 0))
    )
    if not role.first:
        operands.append(before)
        specs.append(whole)
    scratch = deposit_scratch(together, lines)
    if role.last:
        shapes = ((S, CZ, own_rows, Y), (3, S, CZ, own_rows, Y))
        out_shape = tuple(jax.ShapeDtypeStruct(shape, jnp.float32) for shape in shapes)
        out_specs = (hbm, hbm)
        scratch = [
            pltpu.VMEM(grid_shape, jnp.float32),
            pltpu.SMEM((S, S), jnp.float32),
            pltpu.VMEM(shapes[0], jnp.float32),
            pltpu.VMEM(shapes[1], jnp.float32),
            pltpu.SemaphoreType.DMA((1 + 2 * S * CZ,)),
        ] + scratch
    else:
        out_shape = jax.ShapeDtypeStruct(grid_shape, jnp.float32)
        out_specs = whole
    return pl.pallas_call(
        functools.partial(part_kernel, heights, own_rows, role),
        grid=(role.steps,),
        out_shape=out_shape,
        in_specs=specs,
        out_specs=out_specs,
        scratch_shapes=scratch,
        compiler_params=pltpu.CompilerParams(vmem_limit_bytes=40 << 20),
        name="grid_fields" if role.last else "deposit_first" if role.first else "deposit_more",
    )(*operands)


def deposit_scratch(lists, lines):
    return [
        pltpu.VMEM((lists * lines, LINE), jnp.int32),
        pltpu.VMEM((lists * lines, LINE), jnp.float32),
        pltpu.VMEM((2 * TARGETS, lists * lines, LINE), jnp.float32),
        pltpu.VMEM((max(lists, 8), LINE), jnp.int32),
        pltpu.SMEM((max(lists, 8), LINE), jnp.int32),
        pltpu.SemaphoreType.DMA,
    ]


def turned(block, axis, by):
    count = lax.axis_size(axis)
    return lax.ppermute(block, axis, [(i, (i + by) % count) for i in range(count)])


def on_device(dest_slab, local_cell, species, bead_mass, rise_fraction, chi_matrix):
    bead_count = local_cell.shape[0]
    slab_count = lax.axis_size("slab")
    group_count = lax.axis_size(("beads", "sub"))
    heights = slab_count * CZ
    own_rows = X // group_count
    scale = CZ * X * Y / (bead_count * group_count)
    lines = bead_count // LINE
    list_lines = 3 * lines + META
    vmem = pl.BlockSpec(memory_space=pltpu.VMEM)
    beads = [
        pltpu.with_memory_space_constraint(x.reshape(lines, LINE), pltpu.MemorySpace.HBM)
        for x in (dest_slab, local_cell, species, bead_mass, rise_fraction)
    ]
    block = pl.pallas_call(
        functools.partial(sort_kernel, heights, scale),
        out_shape=jax.ShapeDtypeStruct((list_lines, LINE), jnp.float32),
        in_specs=[pl.BlockSpec(memory_space=pl.ANY)] * 5,
        out_specs=vmem,
        scratch_shapes=[pltpu.VMEM((lines, LINE), x.dtype) for x in beads]
        + [pltpu.SemaphoreType.DMA((5,))],
        compiler_params=pltpu.CompilerParams(vmem_limit_bytes=32 << 20),
        name="sort_beads",
    )(*beads)
    if slab_count > 8:
        column = [lax.all_gather(block, "slab")]
    else:
        steps = sorted(range(1, slab_count), key=lambda k: min(k, slab_count - k))
        column = [x[None] for x in [block] + [turned(block, "slab", k) for k in steps]]
    others = [turned(x, "beads", k) for k in range(1, lax.axis_size("beads")) for x in column]
    column = jnp.concatenate(column)
    others = jnp.concatenate(others)
    grid = deposit_call(heights, own_rows, column, None, None)
    half = jnp.concatenate([column, others])
    half, grid = lax.optimization_barrier((half, grid))
    far = jnp.concatenate([turned(half, "sub", k) for k in range(1, lax.axis_size("sub"))])
    grid = deposit_call(heights, own_rows, others, grid, None)
    return deposit_call(heights, own_rows, far, grid, chi_matrix)


def solution(mesh):
    placed = (
        P(("runs", "slab", "beads", "sub"), None),
        P(("runs", "slab", "beads", "sub")),
        P(("runs", "slab", "beads", "sub")),
        P(("runs", "slab", "beads", "sub")),
        P(("runs", "slab", "beads", "sub")),
        P(),
    )
    return jax.shard_map(
        on_device,
        mesh=mesh,
        in_specs=placed,
        out_specs=(
            P("runs", "slab", ("beads", "sub"), None),
            P(None, "runs", "slab", ("beads", "sub"), None),
        ),
        check_vma=False,
    )
```

```python
import functools

import jax
import jax.numpy as jnp
from jax import lax
from jax.experimental import pallas as pl
from jax.experimental.pallas import tpu as pltpu
from jax.sharding import PartitionSpec as P

S = 4
X = 256
Y = 128
CZ = 2

compress = 0.5

BUCKET = 8
BUCKETS = X // BUCKET
RIM = 4
LINE = 128
WINDOW = 2 * BUCKET
TARGETS = CZ + 2
META = 8
GROUP = 4
SORT_GROUP = 2

NT = (((1,), (1,)), ((), ()))


def pieces_of(values):
    parts = []
    for _ in range(2):
        part = values.astype(jnp.bfloat16)
        parts.append(part)
        values = values - part.astype(jnp.float32)
    parts.append(values.astype(jnp.bfloat16))
    return parts


def sort_kernel(heights, scale, *refs):
    sources, out_ref, targets, sems = refs[:5], refs[5], refs[6:11], refs[11]
    copies = [
        pltpu.make_async_copy(source, target, sems.at[i])
        for i, (source, target) in enumerate(zip(sources, targets))
    ]
    for copy in copies:
        copy.start()
    dest_ref, cell_ref, species_ref, mass_ref, rise_ref = targets
    lines = cell_ref.shape[0]
    places = lines * LINE
    halves = lines // 2
    copies[1].wait()
    cell = cell_ref[...]
    row = (cell // Y) & (X - 1)
    bucket = ((row + RIM) & (X - 1)) // BUCKET
    member_iota = lax.broadcasted_iota(jnp.int32, (BUCKETS, LINE), 0)
    members = [
        jnp.where(bucket[i : i + 1, :] == member_iota, 1.0, 0.0) for i in range(lines)
    ]
    pairs = [jnp.concatenate(members[i : i + 2], 1) for i in range(0, lines, 2)]
    stacked = jnp.concatenate(pairs, 0).astype(jnp.bfloat16)
    source = lax.broadcasted_iota(jnp.int32, (2 * LINE, 3 * LINE), 0)
    target = lax.broadcasted_iota(jnp.int32, (2 * LINE, 3 * LINE), 1)
    before = jnp.where(source < target, 1.0, 0.0).astype(jnp.bfloat16)
    counted = jnp.dot(stacked, before, preferred_element_type=jnp.float32)
    total = jnp.zeros((BUCKETS, LINE), jnp.float32)
    ranks = []
    for i in range(lines // 2):
        rows = slice(i * BUCKETS, (i + 1) * BUCKETS)
        ranks.append(counted[rows, :LINE] + total)
        ranks.append(counted[rows, LINE : 2 * LINE] + total)
        total = total + counted[rows, 2 * LINE :]
    start = total
    shift = 1
    while shift < BUCKETS:
        start = start + jnp.where(member_iota >= shift, pltpu.roll(start, shift, 0), 0.0)
        shift *= 2
    start = start - total
    lane = lax.broadcasted_iota(jnp.int32, (BUCKETS, LINE), 1)
    starts = jnp.sum(jnp.where(member_iota == lane, start, 0.0), 0, keepdims=True)
    starts = jnp.where(lane[:1] < BUCKETS, starts, float(places))
    for i in (0, 2, 3, 4):
        copies[i].wait()
    height = dest_ref[...] * CZ + cell // (X * Y)
    key = (species_ref[...] * heights + height) * (X * Y) + (cell & (X * Y - 1))
    mass = mass_ref[...] * scale
    lower = mass * (1.0 - rise_ref[...])
    upper = mass * rise_ref[...]
    parts = [part.astype(jnp.float32) for part in (key // 65536, (key // 256) & 255, key & 255)]
    parts += [part.astype(jnp.float32) for part in pieces_of(lower) + pieces_of(upper)]
    half_iota = lax.broadcasted_iota(jnp.int32, (halves, LINE), 0)
    slot_iota = lax.broadcasted_iota(jnp.int32, (2 * LINE, LINE), 0).astype(jnp.float32).astype(jnp.bfloat16)
    one, zero = jnp.bfloat16(1), jnp.bfloat16(0)
    placed = 0.0
    for first in range(0, lines, SORT_GROUP):
        lefts, rights = [], []
        for i in range(first, first + SORT_GROUP):
            place = jnp.sum(members[i] * (ranks[i] + start), 0, keepdims=True).astype(jnp.int32)
            hit = half_iota == place // (2 * LINE)
            lefts.append(
                jnp.concatenate([jnp.where(hit, part[i : i + 1, :], 0.0) for part in parts], 0)
            )
            slot = jnp.broadcast_to((place & (2 * LINE - 1)).astype(jnp.float32), (2 * LINE, LINE))
            rights.append(jnp.where(slot.astype(jnp.bfloat16) == slot_iota, one, zero))
        placed = placed + lax.dot_general(
            jnp.concatenate(lefts, 1).astype(jnp.bfloat16),
            jnp.concatenate(rights, 1),
            NT,
            preferred_element_type=jnp.float32,
        )

    def part_of(n):
        return placed[n * halves : (n + 1) * halves]

    sorted_values = (
        part_of(0) * 65536.0 + part_of(1) * 256.0 + part_of(2),
        part_of(3) + part_of(4) + part_of(5),
        part_of(6) + part_of(7) + part_of(8),
    )
    for n, value in enumerate(sorted_values):
        out_ref[n * lines : n * lines + halves] = value[:, :LINE]
        out_ref[n * lines + halves : (n + 1) * lines] = value[:, LINE:]
    out_ref[3 * lines : 3 * lines + META] = jnp.broadcast_to(starts, (META, LINE))


def shares_of(lower, upper, height, first, heights):
    shares = (
        0.0625 * lower,
        0.25 * lower + 0.0625 * upper,
        0.375 * lower + 0.25 * upper,
        0.25 * lower + 0.375 * upper,
        0.0625 * lower + 0.25 * upper,
        0.0625 * upper,
    )
    none = jnp.zeros_like(lower)
    if heights == 8:
        turn = (first + 2 + heights - height) & 7
        kept = list(shares) + [none, none]
        for bit, length in ((4, 7), (2, 5), (1, 4)):
            chosen = (turn & bit) != 0
            kept = [
                jnp.where(chosen, kept[(i + bit) % 8], kept[i]) for i in range(length)
            ]
        return kept
    amounts = []
    for n in range(TARGETS):
        above = (first + n + 2 + heights - height) % heights
        amount = none
        for d, share in enumerate(shares):
            amount = jnp.where(above == d, share, amount)
        amounts.append(amount)
    return amounts


def spare_lines(lists):
    return max(2, lists // 2)


def deposit(heights, own_rows, slab, group, lists_ref, before_ref, grid_ref, scratch):
    near_ref, column_ref, amount_ref, starts_ref, starts_smem, sem = scratch
    lists = lists_ref.shape[0]
    lines = (lists_ref.shape[1] - META) // 3
    places = lines * LINE
    halves = lines // 2
    buckets = own_rows // BUCKET + 1
    windows = -(-buckets // 2)

    starts_ref[0:lists] = lists_ref[:, 3 * lines, :].astype(jnp.int32)
    copy = pltpu.make_async_copy(starts_ref, starts_smem, sem)
    copy.start()
    first_row = group * own_rows - RIM

    def spread(i, carry):
        key = lists_ref[i, 0:lines, :].astype(jnp.int32)
        lower = lists_ref[i, lines : 2 * lines, :]
        upper = lists_ref[i, 2 * lines : 3 * lines, :]
        spot = pl.ds(pl.multiple_of(i * lines, lines), lines)
        plane = key // (X * Y)
        species = plane // heights
        height = plane - species * heights
        row = (key // Y) & (X - 1)
        near_ref[spot, :] = ((row - first_row) & (X - 1)) + (species // 2) * 1024
        column_ref[spot, :] = ((key & (Y - 1)) + (species & 1) * Y).astype(jnp.float32)
        for n, amount in enumerate(shares_of(lower, upper, height, slab * CZ - 1, heights)):
            high = amount.astype(jnp.bfloat16).astype(jnp.float32)
            amount_ref[2 * n, spot, :] = high
            amount_ref[2 * n + 1, spot, :] = amount - high
        return carry

    lax.fori_loop(0, lists, spread, 0, unroll=2)
    copy.wait()

    near_iota = lax.broadcasted_iota(jnp.int32, (2 * WINDOW, LINE), 0)
    near_iota = jnp.where(near_iota >= WINDOW, near_iota + (1024 - WINDOW), near_iota)
    column_iota = lax.broadcasted_iota(jnp.int32, (2 * Y, LINE), 0).astype(jnp.float32).astype(jnp.bfloat16)
    one, zero = jnp.bfloat16(1), jnp.bfloat16(0)

    def operands_of(i, line, base):
        at = pl.ds(i * lines + (line & 1) * halves + ((line & (lines - 1)) >> 1), 1)
        hit = jnp.where(near_ref[at, :] - base == near_iota, 1.0, 0.0).astype(jnp.bfloat16)
        left = [
            hit * jnp.broadcast_to(amount_ref[n, at, :], hit.shape).astype(jnp.bfloat16)
            for n in range(2 * TARGETS)
        ]
        column = jnp.broadcast_to(column_ref[at, :], (2 * Y, LINE)).astype(jnp.bfloat16)
        return jnp.concatenate(left, 0), jnp.where(column == column_iota, one, zero)

    def add_product(window, entries, base_ref):
        got = 0.0
        for g in range(0, len(entries), GROUP):
            pairs = [operands_of(*entry) for entry in entries[g : g + GROUP]]
            got = got + lax.dot_general(
                jnp.concatenate([pair[0] for pair in pairs], 1),
                jnp.concatenate([pair[1] for pair in pairs], 1),
                NT,
                preferred_element_type=jnp.float32,
            )
        for n in range(TARGETS):
            for half in range(2):
                high = (2 * n * 2 + half) * WINDOW
                low = ((2 * n + 1) * 2 + half) * WINDOW
                rows = slice(window * WINDOW, (window + 1) * WINDOW)
                value = got[high : high + WINDOW] + got[low : low + WINDOW]
                if base_ref is not None:
                    value = value + base_ref[n, half, rows, :]
                grid_ref[n, half, rows, :] = value

    never = 8192
    spare = spare_lines(lists)

    def range_of(window):
        usual = min(2, buckets - 2 * window) + 1
        low = group * (own_rows // BUCKET) + 2 * window
        high = low + usual - 1
        wrapped = jnp.where(high > BUCKETS, BUCKETS, 0)
        lead = jnp.where(high > BUCKETS, places, 0)

        def span_of(i):
            begin = starts_smem[i, low]
            end = starts_smem[i, high - wrapped] + lead
            first = begin // LINE
            count = jnp.where(end > begin, (end + (LINE - 1)) // LINE - first, 0)
            return first, jnp.minimum(count, lines)

        return usual, span_of

    flags = []
    for window in range(windows):
        usual, span_of = range_of(window)
        base = window * WINDOW
        spare_list = [jnp.int32(0)] * spare
        spare_line = [jnp.int32(0)] * spare
        spare_base = [jnp.int32(never)] * spare
        used = jnp.int32(0)
        most = jnp.int32(0)
        entries = []
        for i in range(lists):
            first, count = span_of(i)
            for t in range(usual):
                entries.append((i, first + t, jnp.where(t < count, base, never)))
            over = count > usual
            for k in range(spare):
                mine = over & (used == k)
                spare_list[k] = jnp.where(mine, i, spare_list[k])
                spare_line[k] = jnp.where(mine, first + usual, spare_line[k])
                spare_base[k] = jnp.where(mine, base, spare_base[k])
            used = used + jnp.where(over, 1, 0)
            most = jnp.maximum(most, count)
        for k in range(spare):
            entries.append((spare_list[k], spare_line[k], spare_base[k]))
        add_product(window, entries, before_ref)
        flags.append((used > spare) | (most > usual + 1))

    def rest_of_window(window):
        usual, span_of = range_of(window)
        base = window * WINDOW

        def rest_of(i, before):
            first, count = span_of(i)
            over = count > usual
            done = usual + jnp.where(over & (before < spare), 1, 0)

            def four_lines(turn, carry):
                ahead = [done + turn * 4 + k for k in range(4)]
                entries = [(i, first + t, jnp.where(t < count, base, never)) for t in ahead]
                add_product(window, entries, grid_ref)
                return carry

            lax.fori_loop(0, (count - done + 3) // 4, four_lines, 0)
            return before + jnp.where(over, 1, 0)

        lax.fori_loop(0, lists, rest_of, jnp.int32(0))

    @pl.when(functools.reduce(jnp.logical_or, flags))
    def _():
        for window in range(windows):
            pl.when(flags[window])(functools.partial(rest_of_window, window))


def fields(
    own_rows, chi_ref, grid_ref, layer_ref, potential_ref, force_ref, potential_hbm, force_hbm, sems
):
    rows = own_rows + 2

    def smooth_of(n, b):
        lanes = slice((b % 2) * Y, (b % 2 + 1) * Y)

        def shifted(k):
            return grid_ref[n, b // 2, RIM - 3 + k : RIM - 3 + k + rows, lanes]

        value = (
            0.375 * shifted(2) + 0.25 * (shifted(1) + shifted(3)) + 0.0625 * (shifted(0) + shifted(4))
        )
        close = pltpu.roll(value, 1, 1) + pltpu.roll(value, Y - 1, 1)
        far = pltpu.roll(value, 2, 1) + pltpu.roll(value, Y - 2, 1)
        return 0.375 * value + 0.25 * close + 0.0625 * far

    factors = [
        [0.5 * (chi_ref[a, b] + chi_ref[b, a]) + 1.0 / compress for b in range(S)] for a in range(S)
    ]
    smooth = [[smooth_of(n, b) for b in range(S)] for n in range(TARGETS)]
    copies = []
    for a in range(S):
        for n in range(TARGETS):
            value = -1.0 / compress
            for b in range(S):
                value = value + factors[a][b] * smooth[n][b]
            layer_ref[a, n, 0:rows] = value
        for z in range(CZ):
            own = layer_ref[a, z + 1, 1 : 1 + own_rows]
            potential_ref[a, z] = own
            force_ref[0, a, z] = (
                layer_ref[a, z, 1 : 1 + own_rows] - layer_ref[a, z + 2, 1 : 1 + own_rows]
            ) * 0.5
            force_ref[1, a, z] = (
                layer_ref[a, z + 1, 0:own_rows] - layer_ref[a, z + 1, 2 : 2 + own_rows]
            ) * 0.5
            force_ref[2, a, z] = (pltpu.roll(own, 1, 1) - pltpu.roll(own, Y - 1, 1)) * 0.5
        copies += [
            pltpu.make_async_copy(potential_ref.at[a], potential_hbm.at[a], sems.at[1 + 2 * a]),
            pltpu.make_async_copy(force_ref.at[:, a], force_hbm.at[:, a], sems.at[2 + 2 * a]),
        ]
        copies[-2].start()
        copies[-1].start()
    for copy in copies:
        copy.wait()


def part_kernel(heights, own_rows, role, *refs):
    step = pl.program_id(0) if role.steps > 1 else 0
    refs = list(refs)
    chi_hbm = refs.pop(0) if role.last else None
    lists_ref = refs.pop(0)
    before_ref = None if role.first else refs.pop(0)
    if role.last:
        potential_ref, force_ref = refs.pop(0), refs.pop(0)
    grid_ref = refs.pop(0)
    if role.last:
        chi_ref, layer_ref, potential_vmem, force_vmem, sems = refs[:5]
        del refs[:5]
        chi_copy = pltpu.make_async_copy(chi_hbm, chi_ref, sems.at[0])
        pl.when(step == 0)(chi_copy.start)

    if role.steps > 1:

        @pl.when(step == 0)
        def _():
            grid_ref[...] = jnp.zeros_like(grid_ref) if role.first else before_ref[...]

        before_ref = grid_ref

    deposit(heights, own_rows, lax.axis_index("slab"), lax.axis_index(("beads", "sub")), lists_ref, before_ref, grid_ref, refs)

    if role.last:

        @pl.when(step == role.steps - 1)
        def _():
            chi_copy.wait()
            fields(
                own_rows, chi_ref, grid_ref, layer_ref, potential_vmem, force_vmem, potential_ref, force_ref, sems
            )


class Role:
    def __init__(self, first, last, steps):
        self.first, self.last, self.steps = first, last, steps


def deposit_call(heights, own_rows, lists, before, chi):
    total, list_lines, _ = lists.shape
    lines = (list_lines - META) // 3
    together = max(n for n in range(1, 9) if total % n == 0)
    role = Role(before is None, chi is not None, total // together)
    whole = pl.BlockSpec(memory_space=pltpu.VMEM)
    hbm = pl.BlockSpec(memory_space=pl.ANY)
    windows = -(-(own_rows // BUCKET + 1) // 2)
    grid_shape = (TARGETS, 2, windows * WINDOW, 2 * Y)
    operands, specs = [], []
    if role.last:
        operands.append(pltpu.with_memory_space_constraint(chi, pltpu.MemorySpace.HBM))
        specs.append(hbm)
    operands.append(lists)
    specs.append(
        whole if role.steps == 1 else pl.BlockSpec((together, list_lines, LINE), lambda i: (i, 0, 0))
    )
    if not role.first:
        operands.append(before)
        specs.append(whole)
    scratch = deposit_scratch(together, lines)
    if role.last:
        shapes = ((S, CZ, own_rows, Y), (3, S, CZ, own_rows, Y))
        out_shape = tuple(jax.ShapeDtypeStruct(shape, jnp.float32) for shape in shapes)
        out_specs = (hbm, hbm)
        scratch = [
            pltpu.VMEM(grid_shape, jnp.float32),
            pltpu.SMEM((S, S), jnp.float32),
            pltpu.VMEM((S, TARGETS, own_rows + 8, Y), jnp.float32),
            pltpu.VMEM(shapes[0], jnp.float32),
            pltpu.VMEM(shapes[1], jnp.float32),
            pltpu.SemaphoreType.DMA((1 + 2 * S,)),
        ] + scratch
    else:
        out_shape = jax.ShapeDtypeStruct(grid_shape, jnp.float32)
        out_specs = whole
    return pl.pallas_call(
        functools.partial(part_kernel, heights, own_rows, role),
        grid=(role.steps,),
        out_shape=out_shape,
        in_specs=specs,
        out_specs=out_specs,
        scratch_shapes=scratch,
        compiler_params=pltpu.CompilerParams(vmem_limit_bytes=40 << 20),
        name="grid_fields" if role.last else "deposit_first" if role.first else "deposit_more",
    )(*operands)


def deposit_scratch(lists, lines):
    return [
        pltpu.VMEM((lists * lines, LINE), jnp.int32),
        pltpu.VMEM((lists * lines, LINE), jnp.float32),
        pltpu.VMEM((2 * TARGETS, lists * lines, LINE), jnp.float32),
        pltpu.VMEM((max(lists, 8), LINE), jnp.int32),
        pltpu.SMEM((max(lists, 8), LINE), jnp.int32),
        pltpu.SemaphoreType.DMA,
    ]


def turned(block, axis, by):
    count = lax.axis_size(axis)
    return lax.ppermute(block, axis, [(i, (i + by) % count) for i in range(count)])


def on_device(dest_slab, local_cell, species, bead_mass, rise_fraction, chi_matrix):
    bead_count = local_cell.shape[0]
    slab_count = lax.axis_size("slab")
    group_count = lax.axis_size(("beads", "sub"))
    heights = slab_count * CZ
    own_rows = X // group_count
    scale = CZ * X * Y / (bead_count * group_count)
    lines = bead_count // LINE
    list_lines = 3 * lines + META
    vmem = pl.BlockSpec(memory_space=pltpu.VMEM)
    beads = [
        pltpu.with_memory_space_constraint(x.reshape(lines, LINE), pltpu.MemorySpace.HBM)
        for x in (dest_slab, local_cell, species, bead_mass, rise_fraction)
    ]
    block = pl.pallas_call(
        functools.partial(sort_kernel, heights, scale),
        out_shape=jax.ShapeDtypeStruct((list_lines, LINE), jnp.float32),
        in_specs=[pl.BlockSpec(memory_space=pl.ANY)] * 5,
        out_specs=vmem,
        scratch_shapes=[pltpu.VMEM((lines, LINE), x.dtype) for x in beads]
        + [pltpu.SemaphoreType.DMA((5,))],
        compiler_params=pltpu.CompilerParams(vmem_limit_bytes=32 << 20),
        name="sort_beads",
    )(*beads)
    if slab_count > 8:
        column = [lax.all_gather(block, "slab")]
    else:
        steps = sorted(range(1, slab_count), key=lambda k: (-min(k, slab_count - k), -k))
        column = [x[None] for x in [block] + [turned(block, "slab", k) for k in steps]]
    others = [turned(x, "beads", k) for k in range(1, lax.axis_size("beads")) for x in column]
    early = jnp.concatenate(column + others[:1])
    late = jnp.concatenate(others[1:])
    grid = deposit_call(heights, own_rows, early, None, None)
    half = jnp.concatenate([early, late])
    half, grid = lax.optimization_barrier((half, grid))
    far = jnp.concatenate([turned(half, "sub", k) for k in range(1, lax.axis_size("sub"))])
    grid = deposit_call(heights, own_rows, late, grid, None)
    return deposit_call(heights, own_rows, far, grid, chi_matrix)


def solution(mesh):
    placed = (
        P(("runs", "slab", "beads", "sub"), None),
        P(("runs", "slab", "beads", "sub")),
        P(("runs", "slab", "beads", "sub")),
        P(("runs", "slab", "beads", "sub")),
        P(("runs", "slab", "beads", "sub")),
        P(),
    )
    return jax.shard_map(
        on_device,
        mesh=mesh,
        in_specs=placed,
        out_specs=(
            P("runs", "slab", ("beads", "sub"), None),
            P(None, "runs", "slab", ("beads", "sub"), None),
        ),
        check_vma=False,
    )
```
